128 devices in a mesh: tm: 16 (over x, z), rows: 8 (over y, core).
Axes of the slice: x: 4, y: 4, z: 4, core: 2. Of those that a mesh axis runs over, the one named last changes fastest.
Arguments:
- video: bfloat16 [256, 32, 32, 512], P('tm', 'rows'), may hold values from -6 to 6
- video_ids: int32 [256], replicated, may hold values from 0 to 15, never falling along the last dimension, each value on 1 to 32 neighbouring positions
- w_space: bfloat16 [9, 512, 512], replicated, may hold values from -0.09375 to 0.09375
- w_time: bfloat16 [3, 512, 512], replicated, may hold values from -0.15625 to 0.15625
- spatial_attn: bfloat16 [4, 512, 512], replicated, may hold values from -2 to 2, as said below
- time_attn: bfloat16 [4, 512, 512], replicated, may hold values from -2 to 2, as said below
Outputs:
- mixed: bfloat16 [256, 32, 32, 512], P(None, 'rows', 'tm')
The draws below stay inside these ranges and needn't reach their ends.
Inputs may be any that keep to these rules, and one draw needn't show every extreme that they name: `spatial_attn`: Query, key, value and output projections stacked in this order. `time_attn`: Query, key, value and output projections stacked in this order.
All inputs are finite; a program needn't handle non-finite values.
Results may differ from the reference program's by a relative error of at most 0.024.
The reference program's roundings to bfloat16 on the way count: a program that leaves them out, or rounds other values in their place, can miss the bound.
Values may be sent and summed in bfloat16 or wider, within the bound.
No kernel may reach another device: no remote copies, remote signals or barrier semaphores. Data moves between devices by JAX's collectives and lax.ppermute only.
A program may use at most 128 MiB of HBM per device.

```python
import math
import jax
import jax.numpy as jnp
import numpy as np
from jax import lax

C = 512
H = 32
W = 32
GROUPS = 32
LONGEST = 32
FRAMES = 256
VIDEOS = 16


def stacked_projections(key):
    first = jax.random.fold_in(key, 0)
    weights = jax.random.normal(first, (4, C, C), jnp.float32) / jnp.sqrt(jnp.float32(C))
    return jnp.clip(weights, -2.0, 2.0).astype(jnp.bfloat16)


def draw_spatial_attn(key, part):
    return stacked_projections(jax.random.fold_in(key, 101))


def draw_time_attn(key, part):
    return stacked_projections(jax.random.fold_in(key, 202))


def block_levels(stream_key, dims, pieces, smallest, top_value):
    gain, own = 1.0, jax.random.fold_in(stream_key, 6)
    for dim, blocks in pieces:
        draws = jnp.exp(jax.random.uniform(jax.random.fold_in(own, dim), (blocks,), jnp.float32, smallest / len(pieces), top_value / len(pieces)))
        gain = gain * jnp.repeat(draws, dims[dim] // blocks).reshape([-1 if axis == dim else 1 for axis in range(len(dims))])
    return gain


def split_up(amount, total, reach, slope):
    weights = [(1 << 20) // math.isqrt(grade ** slope) + 1 for grade in range(2, amount + 1)]
    surplus, counts = total - reach - (amount - 1), [1] * (amount - 1)
    while surplus > 0:
        movable = [i for i in range(amount - 1) if counts[i] < reach]
        pool, left = sum([weights[i] for i in movable]), surplus
        for i in movable:
            addition = min(reach - counts[i], max(1, left * weights[i] // pool), surplus)
            counts[i] = counts[i] + addition
            surplus = surplus - addition
    return np.array([reach] + counts)


def ragged(own_key, amount, total, bound, lean):
    if amount == 2:
        one = jax.random.randint(own_key, (), max(1, total - bound), min(bound, total - 1) + 1)
        return jnp.stack([one, total - one])
    lengths = jnp.asarray(split_up(amount, total, bound, lean), jnp.int32)
    twos = (amount - 1) // 2
    source_of, taker = lengths[1:1 + 2 * twos:2], lengths[2:2 + 2 * twos:2]
    slack = jnp.minimum(source_of - 1, bound - taker)
    passed = jax.random.randint(jax.random.fold_in(own_key, 1), (twos,), 0, 1 << 20) % (slack + 1)
    lengths = lengths.at[1:1 + 2 * twos:2].set(source_of - passed).at[2:2 + 2 * twos:2].set(taker + passed)
    return lengths[jax.random.permutation(jax.random.fold_in(own_key, 2), amount)]


def normal_values(rng, shape, scale, limit, cuts=(), kind=jnp.bfloat16):
    values = scale * jax.random.normal(rng, shape, jnp.float32)
    if cuts:
        values = values * block_levels(rng, shape, cuts, -0.22, 0.18)
    return jnp.clip(values, -limit, limit).astype(kind)


def setup_inputs(seed: int = 0) -> dict:
    seeds = jax.random.split(jax.random.key(seed), 7)
    video = normal_values(seeds[0], (FRAMES, H, W, C), 1.0, 6.0, ((0, 16), (1, 8)))
    video_ids = jnp.searchsorted(jnp.cumsum(ragged(seeds[1], VIDEOS, FRAMES, LONGEST, 2)), jnp.arange(FRAMES), side="right").astype(jnp.int32)
    w_space = normal_values(seeds[2], (9, C, C), (9 * C) ** -0.5, 0.09375)
    w_time = normal_values(seeds[3], (3, C, C), (3 * C) ** -0.5, 0.15625)
    spatial_attn = draw_spatial_attn(jax.random.fold_in(seeds[6], 71), 0)
    time_attn = draw_time_attn(jax.random.fold_in(seeds[6], 71), 0)
    return {"video": video, "video_ids": video_ids, "w_space": w_space, "w_time": w_time, "spatial_attn": spatial_attn, "time_attn": time_attn}


epsilon = 1e-06
masked_score = -1e+30

def space_conv(video, weights):
    frame_count, row_count, col_count, channel_width = video.shape
    widened = jnp.pad(video, ((0, 0), (1, 1), (1, 1), (0, 0)))
    summed = jnp.zeros((frame_count * row_count * col_count, channel_width), jnp.float32)
    for row_shift in range(3):
        for col_shift in range(3):
            window = widened[:, row_shift:row_shift + row_count, col_shift:col_shift + col_count, :]
            summed = summed + jnp.dot(window.reshape(-1, channel_width), weights[row_shift * 3 + col_shift], preferred_element_type=jnp.float32)
    return summed.reshape(video.shape)

def time_taps(hidden, video_ids):
    frame_total = hidden.shape[0]
    frame_index = jnp.arange(frame_total, dtype=jnp.int32)
    back_one = jnp.maximum(frame_index - 1, 0).astype(jnp.int32)
    back_two = jnp.maximum(frame_index - 2, 0).astype(jnp.int32)
    prev_one = jnp.where((frame_index >= 1) & (video_ids[back_one] == video_ids), back_one, frame_index)
    prev_two = jnp.where((frame_index >= 2) & (video_ids[back_two] == video_ids), back_two, prev_one)
    return (jnp.take(hidden, prev_one, axis=0), jnp.take(hidden, prev_two, axis=0))

def group_norm(tokens, groups):
    batch_size, length, channel_width = tokens.shape
    per_group = channel_width // groups
    values = tokens.astype(jnp.float32)
    group_sums = lax.optimization_barrier(jnp.sum(values, axis=1)).reshape(batch_size, groups, per_group).sum(axis=2)
    squares = lax.optimization_barrier(jnp.sum(values * values, axis=1)).reshape(batch_size, groups, per_group).sum(axis=2)
    entries = length * per_group
    average = group_sums / entries
    spread = squares / entries - average * average
    inverse = lax.rsqrt(spread + epsilon)
    average_full = jnp.repeat(average, per_group, axis=1)[:, None, :]
    inverse_full = jnp.repeat(inverse, per_group, axis=1)[:, None, :]
    return ((values - average_full) * inverse_full).astype(jnp.bfloat16)

def project(normed, weights):
    shape_in = normed.shape
    channel_width = shape_in[-1]
    flattened = normed.reshape(-1, channel_width)
    outputs = [jnp.dot(flattened, weights[index], preferred_element_type=jnp.float32).astype(jnp.bfloat16).reshape(shape_in) for index in range(3)]
    return (outputs[0], outputs[1], outputs[2])

def frame_attention(tokens, normed, weights):
    channel_width = tokens.shape[-1]
    query_rows, resident_keys, resident_values = project(normed, weights)
    attention_logits = jnp.einsum('edm,efm->edf', query_rows.astype(jnp.float32), resident_keys.astype(jnp.float32)) * channel_width ** (-0.5)
    top = lax.optimization_barrier(jnp.max(attention_logits, axis=-1, keepdims=True))
    raised = jnp.exp(attention_logits - top)
    attention_probs = (raised / lax.optimization_barrier(jnp.sum(raised, axis=-1, keepdims=True))).astype(jnp.bfloat16)
    mixed_output = jnp.einsum('lup,lpe->lue', attention_probs.astype(jnp.float32), resident_values.astype(jnp.float32)).astype(jnp.bfloat16)
    output = tokens.astype(jnp.float32) + jnp.dot(mixed_output.reshape(-1, channel_width), weights[3], preferred_element_type=jnp.float32).reshape(tokens.shape)
    return output.astype(jnp.bfloat16)

def time_attention(column_block, video_ids, weights):
    frame_total, positions, channel_width = column_block.shape
    values = column_block.astype(jnp.float32)
    average = lax.optimization_barrier(jnp.mean(values, axis=-1, keepdims=True))
    centered = values - average
    spread = lax.optimization_barrier(jnp.mean(centered * centered, axis=-1, keepdims=True))
    normed = (centered * lax.rsqrt(spread + epsilon)).astype(jnp.bfloat16)
    query_rows, resident_keys, resident_values = project(normed, weights)
    attention_logits = jnp.einsum('fpc,gpc->pfg', query_rows.astype(jnp.float32), resident_keys.astype(jnp.float32)) * channel_width ** (-0.5)
    frame_index = jnp.arange(frame_total, dtype=jnp.int32)
    allowed = (frame_index[None, :] <= frame_index[:, None]) & (video_ids[None, :] == video_ids[:, None])
    attention_logits = jnp.where(allowed[None], attention_logits, masked_score)
    top = lax.optimization_barrier(jnp.max(attention_logits, axis=-1, keepdims=True))
    raised = jnp.exp(attention_logits - top)
    attention_probs = (raised / lax.optimization_barrier(jnp.sum(raised, axis=-1, keepdims=True))).astype(jnp.bfloat16)
    mixed_output = jnp.einsum('pfg,gpc->fpc', attention_probs.astype(jnp.float32), resident_values.astype(jnp.float32)).astype(jnp.bfloat16)
    output = values + jnp.dot(mixed_output.reshape(-1, channel_width), weights[3], preferred_element_type=jnp.float32).reshape(column_block.shape)
    return output.astype(jnp.bfloat16)

def reference(video, video_ids, w_space, w_time, spatial_attn, time_attn):
    frame_count, row_count, col_count, channel_width = video.shape
    hidden = jax.nn.silu(space_conv(video, w_space)).astype(jnp.bfloat16)
    prev_one, prev_two = time_taps(hidden, video_ids)
    temporal = jnp.dot(hidden.reshape(-1, channel_width), w_time[0], preferred_element_type=jnp.float32)
    temporal = temporal + jnp.dot(prev_one.reshape(-1, channel_width), w_time[1], preferred_element_type=jnp.float32)
    temporal = temporal + jnp.dot(prev_two.reshape(-1, channel_width), w_time[2], preferred_element_type=jnp.float32)
    conv_out = (video.astype(jnp.float32) + temporal.reshape(video.shape)).astype(jnp.bfloat16)
    tokens = conv_out.reshape(frame_count, row_count * col_count, channel_width)
    normed = group_norm(tokens, GROUPS)

    def one_frame(paired):
        return frame_attention(paired[0][None], paired[1][None], spatial_attn)[0]
    frame_out = lax.map(one_frame, (tokens, normed)).reshape(video.shape)
    columns = jnp.moveaxis(frame_out, 1, 0)

    def one_row(column_block):
        return time_attention(column_block, video_ids, time_attn)
    by_time = lax.map(one_row, columns)
    return jnp.moveaxis(by_time, 0, 1)
```

```python
import functools

import jax
import jax.numpy as jnp
import numpy as np
from jax import lax
from jax.experimental import pallas as pl
from jax.experimental.pallas import tpu as pltpu
from jax.sharding import PartitionSpec as P

GROUPS = 32
EPS = 1e-06
MASKED = -1e30
LOG2E = 1.4426950408889634
BF = jnp.bfloat16
F32 = jnp.float32
VMEM_LIMIT = 56 * 1024 * 1024


def mm(a, b):
    return jnp.dot(a, b, preferred_element_type=F32)


def mm_nt(a, b):
    return lax.dot_general(a, b, (((1,), (1,)), ((), ())), preferred_element_type=F32)


def one_hot_rows(n, source_of):
    out_row = lax.broadcasted_iota(jnp.int32, (n, n), 0)
    in_row = lax.broadcasted_iota(jnp.int32, (n, n), 1)
    return jnp.where(in_row == source_of(out_row), 1.0, 0.0).astype(BF)


def conv_kernel(first, frames, idx_ref, *refs):
    if first:
        (x_ref, up_ref, dn_ref, xp_ref, upp_ref, dnp_ref, w_ref, wt_ref,
         out_ref, tail_ref, ext, acc, hs) = refs
        lead = 2
    else:
        (x_ref, up_ref, dn_ref, hp_ref, w_ref, wt_ref, out_ref, ext, acc, hs) = refs
        lead = 0
    total = frames + lead
    per = 5 if total % 5 == 0 else 4
    rows = per * 128
    step = pl.program_id(0)
    c = x_ref.shape[-1]

    @pl.when(step == 0)
    def _():
        if first:
            ext[0:2, 0:32, :] = upp_ref[...]
            ext[0:2, 32:160, :] = xp_ref[...]
            ext[0:2, 160:192, :] = dnp_ref[...]
        else:
            hs[0:2] = hp_ref[...]
        ext[lead:total, 0:32, :] = up_ref[...]
        ext[lead:total, 32:160, :] = x_ref[...]
        ext[lead:total, 160:192, :] = dn_ref[...]

    def tap(block):
        f0 = block * per
        lhs = jnp.concatenate(
            [ext[f0 : f0 + per, 32 * a : 32 * a + 128, :].reshape(rows, c) for a in range(3)], axis=1
        )
        return mm(lhs, w_ref[:, 0].reshape(3 * c, c))

    def col_is(value):
        row = lax.broadcasted_iota(jnp.int32, (rows, c), 0)
        return (row & 31) == value

    @pl.when(step == 0)
    def _():
        for block in range(total // per):
            y = tap(block)
            acc[block * rows : (block + 1) * rows] = jnp.where(col_is(0), 0.0, pltpu.roll(y, 1, 0))

    @pl.when(step == 1)
    def _():
        for block in range(total // per):
            acc[block * rows : (block + 1) * rows] += tap(block)

    @pl.when(step == 2)
    def _():
        for block in range(total // per):
            y = tap(block)
            y = jnp.where(col_is(31), 0.0, pltpu.roll(y, rows - 1, 0))
            v = acc[block * rows : (block + 1) * rows] + y
            half = 0.5 * v
            hidden = (half + half * jnp.tanh(half)).astype(BF)
            f0 = block * per + 2 - lead
            hs[f0 : f0 + per] = hidden.reshape(per, 128, c)

    @pl.when(step == 3)
    def _():
        order = one_hot_rows(128, lambda o: ((o >> 1) & 3) * 32 + (o >> 3) * 2 + (o & 1))
        weights = wt_ref[...].reshape(3 * c, c)
        per_t = 4
        for f0 in range(0, frames, per_t):
            now = hs[f0 + 2 : f0 + 2 + per_t].reshape(per_t * 128, c)
            one = jnp.concatenate([hs[idx_ref[0, f0 + k]] for k in range(per_t)], axis=0)
            two = jnp.concatenate([hs[idx_ref[1, f0 + k]] for k in range(per_t)], axis=0)
            y = mm(jnp.concatenate([now, one, two], axis=1), weights)
            y = y + x_ref[f0 : f0 + per_t].reshape(per_t * 128, c).astype(F32)
            y = y.astype(BF)
            for k in range(per_t):
                out_ref[f0 + k] = mm(order, y[k * 128 : (k + 1) * 128]).astype(BF)
        if first:
            tail_ref[...] = hs[frames : frames + 2]


def conv_chunk(first, idx, x, halos, w_space, w_time):
    frames, tokens, c = x.shape
    total = frames + (2 if first else 0)
    whole = lambda a: pl.BlockSpec(a.shape, lambda s, i, n=a.ndim: (0,) * n)
    ins = [x, *halos]
    in_specs = [whole(a) for a in ins]
    in_specs.append(pl.BlockSpec((3, 1, c, c), lambda s, i: (0, jnp.minimum(s, 2), 0, 0)))
    in_specs.append(whole(w_time))
    out_shape = [jax.ShapeDtypeStruct((frames, tokens, c), BF)]
    if first:
        out_shape.append(jax.ShapeDtypeStruct((2, tokens, c), BF))
    flops = 2 * total * tokens * 9 * c * c + 2 * frames * tokens * 3 * c * c
    return pl.pallas_call(
        functools.partial(conv_kernel, first, frames),
        out_shape=out_shape,
        grid_spec=pltpu.PrefetchScalarGridSpec(
            num_scalar_prefetch=1,
            grid=(4,),
            in_specs=in_specs,
            out_specs=[whole(o) for o in out_shape],
            scratch_shapes=[
                pltpu.VMEM((total, 192, c), BF),
                pltpu.VMEM((total * tokens, c), F32),
                pltpu.VMEM((frames + 2, tokens, c), BF),
            ],
        ),
        compiler_params=pltpu.CompilerParams(
            dimension_semantics=("arbitrary",), vmem_limit_bytes=VMEM_LIMIT
        ),
        cost_estimate=pl.CostEstimate(flops=flops, bytes_accessed=9 * 2**20, transcendentals=0),
        name="conv_chunk",
    )(idx, *ins, w_space.reshape(3, 3, c, c), w_time)


def softmax_rows(scores, scale):
    top = jnp.max(scores, axis=-1, keepdims=True)
    raised = jnp.exp2((scores - top) * scale)
    return (raised * (1.0 / jnp.sum(raised, axis=-1, keepdims=True))).astype(BF)


def group_sum(v, per_group):
    lane = lax.broadcasted_iota(jnp.int32, v.shape, 1)
    n = v.shape[1]
    d = 1
    while d < per_group:
        v = v + jnp.where((lane & d) == 0, pltpu.roll(v, n - d, 1), pltpu.roll(v, d, 1))
        d *= 2
    return v


def frame_kernel(x_ref, xq_ref, w_ref, out_ref, q_s, k_s, v_s):
    step = pl.program_id(0)
    tokens, c = x_ref.shape
    tile = out_ref.shape[0]

    @pl.when(step == 0)
    def _():
        values = x_ref[...].astype(F32)
        sums = jnp.sum(values, axis=0, keepdims=True)
        squares = jnp.sum(values * values, axis=0, keepdims=True)
        per_group = c // GROUPS
        entries = tokens * per_group
        both = group_sum(jnp.concatenate([sums, squares] * 4, axis=0), per_group) / entries
        average, square = both[0:1], both[1:2]
        inverse = lax.rsqrt(square - average * average + EPS)
        normed = ((values - average) * inverse).astype(BF)
        q_s[...] = mm(normed, w_ref[0]).astype(BF)
        k_s[...] = mm(normed, w_ref[1]).astype(BF)
        v_s[...] = mm(normed, w_ref[2]).astype(BF)

    q = q_s[pl.ds(step * tile, tile), :]
    probs = softmax_rows(mm_nt(q, k_s[...]), c ** (-0.5) * LOG2E)
    mix = mm(probs, v_s[...]).astype(BF)
    out_ref[...] = (xq_ref[...].astype(F32) + mm(mix, w_ref[3])).astype(BF)


def frame_attention(x, weights):
    tokens, c = x.shape
    tile = 256
    return pl.pallas_call(
        frame_kernel,
        out_shape=jax.ShapeDtypeStruct((tokens, c), BF),
        grid=(tokens // tile,),
        in_specs=[
            pl.BlockSpec((tokens, c), lambda s: (0, 0)),
            pl.BlockSpec((tile, c), lambda s: (s, 0)),
            pl.BlockSpec(weights.shape, lambda s: (0, 0, 0)),
        ],
        out_specs=pl.BlockSpec((tile, c), lambda s: (s, 0)),
        scratch_shapes=[pltpu.VMEM((tokens, c), BF)] * 3,
        compiler_params=pltpu.CompilerParams(
            dimension_semantics=("arbitrary",), vmem_limit_bytes=VMEM_LIMIT
        ),
        cost_estimate=pl.CostEstimate(
            flops=8 * tokens * c * c + 4 * tokens * tokens * c,
            bytes_accessed=5 * 2**20,
            transcendentals=tokens * tokens,
        ),
        name="frame_attention",
    )(x, x, weights)


def by_cell(o):
    return (o & 7) * 32 + ((o >> 3) & 3) * 8 + (o >> 5)


def by_frame(o):
    return (o & 7) * 32 + (o >> 3)


def cell_rows(block, order):
    return mm(order, block).astype(BF)


def project_time(x, w_ref):
    values = x.astype(F32)
    average = jnp.mean(values, axis=-1, keepdims=True)
    centered = values - average
    spread = jnp.mean(centered * centered, axis=-1, keepdims=True)
    normed = (centered * lax.rsqrt(spread + EPS)).astype(BF)
    return [mm(normed, w_ref[i]).astype(BF) for i in range(3)]


def qkv_kernel(x_ref, w_ref, xo_ref, q_ref, k_ref, v_ref):
    c = x_ref.shape[-1]
    order = one_hot_rows(256, by_cell)
    x = cell_rows(x_ref[...].reshape(256, c), order)
    q, k, v = project_time(x, w_ref)
    for ref, value in ((xo_ref, x), (q_ref, q), (k_ref, k), (v_ref, v)):
        ref[...] = value.reshape(8, 32, c)


def time_qkv(x, weights):
    r, tc, c = x.shape
    out = jax.ShapeDtypeStruct((8, r * tc // 8, c), BF)
    block = pl.BlockSpec((8, 32, c), lambda s: (0, s, 0))
    return pl.pallas_call(
        qkv_kernel,
        out_shape=[out] * 4,
        grid=(tc // 32,),
        in_specs=[block, pl.BlockSpec(weights.shape, lambda s: (0, 0, 0))],
        out_specs=[block] * 4,
        compiler_params=pltpu.CompilerParams(
            dimension_semantics=("arbitrary",), vmem_limit_bytes=VMEM_LIMIT
        ),
        cost_estimate=pl.CostEstimate(
            flops=6 * r * tc * c * c, bytes_accessed=7 * 2**20, transcendentals=0
        ),
        name="time_qkv",
    )(x, weights)


def time_kernel(x1_ref, bias_ref, w_ref, x0_hbm, q0_hbm, k0_hbm, v0_hbm, out_ref, x_s, q_s, k_s, v_s, m_s, sems):
    c = x1_ref.shape[-1]
    scratch = (x_s, q_s, k_s, v_s)
    copies = [
        pltpu.make_async_copy(src, dst.at[:, 0:128], sems.at[i])
        for i, (src, dst) in enumerate(zip((x0_hbm, q0_hbm, k0_hbm, v0_hbm), scratch))
    ]
    for copy in copies:
        copy.start()
    order = one_hot_rows(256, by_cell)
    for u in range(4):
        x = cell_rows(x1_ref[:, 32 * u : 32 * u + 32, :].reshape(256, c), order)
        for ref, value in zip(scratch, [x, *project_time(x, w_ref)]):
            ref[:, 128 + 32 * u : 160 + 32 * u, :] = value.reshape(8, 32, c)
    for copy in copies:
        copy.wait()
    for cell in range(8):
        scores = mm_nt(q_s[cell], k_s[cell]) * (c ** (-0.5) * LOG2E) + bias_ref[...]
        m_s[cell] = mm(softmax_rows(scores, 1.0), v_s[cell]).astype(BF)
    back = one_hot_rows(256, by_frame)
    for chunk in range(2):
        for u in range(4):
            f0 = chunk * 128 + 32 * u
            y = mm(m_s[:, f0 : f0 + 32, :].reshape(256, c), w_ref[3])
            y = (y + x_s[:, f0 : f0 + 32, :].reshape(256, c).astype(F32)).astype(BF)
            y = mm(back, y).astype(BF)
            out_ref[4 * u : 4 * u + 4, chunk * 64 : chunk * 64 + 64, :] = y.reshape(4, 64, c)


def time_finish(x1, bias, weights, parts):
    r, tc, c = x1.shape
    vmem = pl.BlockSpec(memory_space=pltpu.VMEM)
    hbm = pl.BlockSpec(memory_space=pl.ANY)
    return pl.pallas_call(
        time_kernel,
        out_shape=jax.ShapeDtypeStruct((16, 128, c), BF),
        in_specs=[vmem] * 3 + [hbm] * 4,
        out_specs=vmem,
        scratch_shapes=[pltpu.VMEM((8, 256, c), BF)] * 5 + [pltpu.SemaphoreType.DMA((4,))],
        compiler_params=pltpu.CompilerParams(vmem_limit_bytes=VMEM_LIMIT),
        cost_estimate=pl.CostEstimate(
            flops=6 * r * tc * c * c + 4 * r * tc * c * c + 8 * 4 * 256 * 256 * c,
            bytes_accessed=10 * 2**20,
            transcendentals=8 * 256 * 256,
        ),
        name="time_finish",
    )(x1, bias, weights, *parts)


def shards(video, video_ids, w_space, w_time, spatial_attn, time_attn):
    frames, rows, cols, c = video.shape
    tm_count, rows_count = lax.axis_size("tm"), lax.axis_size("rows")
    half = frames // 2
    up = [(i, i + 1) for i in range(rows_count - 1)]
    down = [(i + 1, i) for i in range(rows_count - 1)]
    span = [(t, t + 1) for t in range(tm_count - 1)]
    both = ("tm", "rows")
    tokens = rows * cols
    flat = lambda a: a.reshape(a.shape[0], -1, c)

    top, bottom = video[:, 0], video[:, rows - 1]
    late = frames - 2
    halos = [
        (lax.ppermute(bottom[k : k + half], "rows", up), lax.ppermute(top[k : k + half], "rows", down))
        for k in (0, half)
    ]
    prev = lax.ppermute(video[late:], "tm", span)
    diag = lambda moves: [(a * rows_count + i, b * rows_count + j) for a, b in span for i, j in moves]
    prev_up = lax.ppermute(bottom[late:], both, diag(up))
    prev_dn = lax.ppermute(top[late:], both, diag(down))

    ids = jnp.concatenate([jnp.full((2,), -1, jnp.int32), video_ids])
    ids = lax.dynamic_slice_in_dim(ids, lax.axis_index("tm") * frames, frames + 2)
    place = jnp.arange(frames, dtype=jnp.int32) % half
    one = jnp.where(ids[1:-1] == ids[2:], place + 1, place + 2)
    two = jnp.where(ids[:-2] == ids[2:], place, one)
    idx = jnp.stack([one, two])

    x = flat(video)
    conv0, tail = conv_chunk(
        True, idx[:, :half], x[:half], [*halos[0], flat(prev), prev_up, prev_dn], w_space, w_time
    )
    (conv1,) = conv_chunk(False, idx[:, half:], x[half:], [*halos[1], tail], w_space, w_time)

    arrived = []
    for conv in (conv0, conv1):
        frame = lax.all_to_all(conv, "rows", 0, 0, tiled=True).reshape(rows_count * tokens, c)
        out = frame_attention(frame, spatial_attn)
        arrived.append(
            lax.all_to_all(out, ("rows", "tm"), 0, 0, tiled=True).reshape(rows_count, -1, c)
        )

    order = np.arange(frames * tm_count).reshape(tm_count, 2, half).transpose(1, 0, 2).reshape(-1)
    ids_here = video_ids.reshape(tm_count, 2, half).transpose(1, 0, 2).reshape(-1)
    number = jnp.asarray(order, jnp.int32)
    allowed = (number[None, :] <= number[:, None]) & (ids_here[None, :] == ids_here[:, None])
    bias = jnp.where(allowed, 0.0, MASKED).astype(F32)

    parts = time_qkv(arrived[0], time_attn)
    out = time_finish(arrived[1], bias, time_attn, parts)
    return out.reshape(frames * tm_count, rows, cols // tm_count, c)


def solution(mesh):
    in_specs = (P("tm", "rows", None, None), P(), P(), P(), P(), P())
    out_specs = P(None, "rows", "tm", None)
    return jax.shard_map(shards, mesh=mesh, in_specs=in_specs, out_specs=out_specs, check_vma=False)
```

```python
import functools

import jax
import jax.numpy as jnp
from jax import lax
from jax.experimental import pallas as pl
from jax.experimental.pallas import tpu as pltpu
from jax.sharding import PartitionSpec as P

GROUPS = 32
EPS = 1e-06
MASKED = -1e30
LOG2E = 1.4426950408889634
BF = jnp.bfloat16
F32 = jnp.float32
VMEM_LIMIT = 16 * 1024 * 1024


def mm(a, b):
    return jnp.dot(a, b, preferred_element_type=F32)


def mm_nt(a, b):
    return lax.dot_general(a, b, (((1,), (1,)), ((), ())), preferred_element_type=F32)


def one_hot_rows(n, source_of):
    out_row = lax.broadcasted_iota(jnp.int32, (n, n), 0)
    in_row = lax.broadcasted_iota(jnp.int32, (n, n), 1)
    return jnp.where(in_row == source_of(out_row), 1.0, 0.0).astype(BF)


def space_taps(blocks, rows, lhs_of, w_ref, acc, store):
    c = acc.shape[-1]
    row = lax.broadcasted_iota(jnp.int32, (rows, c), 0) & 31

    def product(block, col):
        weights = jnp.concatenate([w_ref[3 * a + col] for a in range(3)], axis=0)
        return mm(lhs_of(block), weights)

    def span(block):
        return slice(block * rows, (block + 1) * rows)

    for block in range(blocks):
        acc[span(block)] = jnp.where(row == 0, 0.0, pltpu.roll(product(block, 0), 1, 0))
    for block in range(blocks):
        acc[span(block)] += product(block, 1)
    for block in range(blocks):
        v = acc[span(block)] + jnp.where(row == 31, 0.0, pltpu.roll(product(block, 2), rows - 1, 0))
        half = 0.5 * v
        store(block, (half + half * jnp.tanh(half)).astype(BF))


def inner_kernel(x_ref, w_ref, out_ref, acc):
    frames, tokens, c = out_ref.shape
    per = 8

    def lhs_of(block):
        f = slice(block * per, (block + 1) * per)
        return jnp.concatenate(
            [x_ref[f, 32 * a : 32 * a + tokens, :].reshape(per * tokens, c) for a in range(3)], axis=1
        )

    def store(block, hidden):
        out_ref[block * per : (block + 1) * per] = hidden.reshape(per, tokens, c)

    space_taps(frames // per, per * tokens, lhs_of, w_ref, acc, store)


def conv_inner(x, w_space):
    frames, tokens, c = x.shape
    rows = frames * (tokens - 64)
    vmem = pl.BlockSpec(memory_space=pltpu.VMEM)
    return pl.pallas_call(
        inner_kernel,
        out_shape=jax.ShapeDtypeStruct((frames, tokens - 64, c), BF),
        in_specs=[vmem] * 2,
        out_specs=vmem,
        scratch_shapes=[pltpu.VMEM((rows, c), F32)],
        compiler_params=pltpu.CompilerParams(vmem_limit_bytes=VMEM_LIMIT),
        cost_estimate=pl.CostEstimate(flops=18 * rows * c * c, bytes_accessed=8 * 2**20, transcendentals=0),
        name="conv_inner",
    )(x, w_space)


def outer_kernel(late, idx_ref, x_ref, up_ref, dn_ref, inner_ref, *refs):
    tokens, c = x_ref.shape[1:]
    count = 10 if late else 6
    frames = slice(6, 16) if late else slice(0, 6)
    if late:
        (w_ref, wt_ref, *outs, lead_ref, tail_ref, acc, hs) = refs
        here = slice(0, 10)
    else:
        (lead_ref, tail_ref, w_ref, wt_ref, *outs, acc, hs) = refs
        here = slice(2, 8)
    rows = count * 64

    hs[here, 32:96, :] = inner_ref[frames]
    if not late:
        hs[0:2] = tail_ref[...]
        hs[8:10] = lead_ref[...]

    def lhs_of(block):
        first = [up_ref[frames], x_ref[frames, 0:32, :], x_ref[frames, 32:64, :]]
        last = [x_ref[frames, 64:96, :], x_ref[frames, 96:128, :], dn_ref[frames]]
        return jnp.concatenate(
            [jnp.concatenate([f, l], axis=0).reshape(rows, c) for f, l in zip(first, last)], axis=1
        )

    def store(block, hidden):
        hidden = hidden.reshape(2, count, 32, c)
        hs[here, 0:32, :] = hidden[0]
        hs[here, 96:128, :] = hidden[1]

    space_taps(1, rows, lhs_of, w_ref, acc, store)

    order = one_hot_rows(128, lambda o: ((o >> 1) & 3) * 32 + (o >> 3) * 2 + (o & 1))
    weights = wt_ref[...].reshape(3 * c, c)
    per = 4
    for s0 in range(0, 8, per):
        taps = [jnp.concatenate([hs[idx_ref[k, s0 + s]] for s in range(per)], axis=0) for k in range(3)]
        y = mm(jnp.concatenate(taps, axis=1), weights)
        for s in range(per):
            own = y[s * tokens : (s + 1) * tokens] + x_ref[idx_ref[3, s0 + s]].astype(F32)
            outs[s0 + s][...] = mm(order, own.astype(BF)).astype(BF)
    if late:
        lead_ref[...] = hs[0:2]
        tail_ref[...] = hs[8:10]


def conv_outer(late, idx, x, up, dn, inner, given, w_space, w_time):
    tokens, c = x.shape[1:]
    count = 10 if late else 6
    ins = [x, up, dn, inner, *given, w_space, w_time]
    vmem = pl.BlockSpec(memory_space=pltpu.VMEM)
    out_shape = [jax.ShapeDtypeStruct((tokens, c), BF)] * 8
    if late:
        out_shape = out_shape + [jax.ShapeDtypeStruct((2, tokens, c), BF)] * 2
    rows = count * 64
    return pl.pallas_call(
        functools.partial(outer_kernel, late),
        out_shape=out_shape,
        in_specs=[pl.BlockSpec(memory_space=pltpu.SMEM)] + [vmem] * len(ins),
        out_specs=[vmem] * len(out_shape),
        scratch_shapes=[pltpu.VMEM((rows, c), F32), pltpu.VMEM((10, tokens, c), BF)],
        compiler_params=pltpu.CompilerParams(vmem_limit_bytes=VMEM_LIMIT),
        cost_estimate=pl.CostEstimate(
            flops=18 * rows * c * c + 48 * tokens * c * c, bytes_accessed=9 * 2**20, transcendentals=0
        ),
        name="conv_outer",
    )(idx, *ins)


def softmax_rows(scores, scale):
    top = jnp.max(scores, axis=-1, keepdims=True)
    raised = jnp.exp2((scores - top) * scale)
    return (raised * (1.0 / jnp.sum(raised, axis=-1, keepdims=True))).astype(BF)


def group_sum(v, per_group):
    lane = lax.broadcasted_iota(jnp.int32, v.shape, 1)
    n = v.shape[1]
    d = 1
    while d < per_group:
        v = v + jnp.where((lane & d) == 0, pltpu.roll(v, n - d, 1), pltpu.roll(v, d, 1))
        d *= 2
    return v


def frame_kernel(pair, place_ref, *refs):
    xs, (w_ref, other_ref, out_ref, q_s, k_s, v_s) = refs[:8], refs[8:]
    block, c = xs[0].shape
    tokens = 8 * block
    per_group = c // GROUPS
    entries = tokens * per_group

    sums, squares = 0.0, 0.0
    for ref in xs:
        values = ref[...].astype(F32)
        sums = sums + jnp.sum(values, axis=0, keepdims=True)
        squares = squares + jnp.sum(values * values, axis=0, keepdims=True)
    both = group_sum(jnp.concatenate([sums, squares] * 4, axis=0), per_group) / entries
    average, square = both[0:1], both[1:2]
    inverse = lax.rsqrt(square - average * average + EPS)
    for s in range(0, 8, 2):
        values = jnp.concatenate([xs[s][...], xs[s + 1][...]], axis=0).astype(F32)
        normed = ((values - average) * inverse).astype(BF)
        for i, ref in enumerate((q_s, k_s, v_s)):
            ref[s * block : (s + 2) * block] = mm(normed, w_ref[i]).astype(BF)
    for s in range(0, 8, 2):
        q = q_s[s * block : (s + 2) * block]
        probs = softmax_rows(mm_nt(q, k_s[...]), c ** (-0.5) * LOG2E)
        y = mm(mm(probs, v_s[...]).astype(BF), w_ref[3])
        for k in range(2):
            part = y[k * block : (k + 1) * block] + xs[s + k][...].astype(F32)
            if pair:
                other = other_ref[place_ref[s + k]].astype(F32).reshape(block // 8, 8, c)
                part = jnp.concatenate([part.reshape(block // 8, 8, c), other], axis=1)
            out_ref[place_ref[s + k]] = part.reshape(-1, c).astype(BF)


def frame_attention(pair, place, xs, weights, other):
    block, c = xs[0].shape
    tokens = 8 * block
    vmem = pl.BlockSpec(memory_space=pltpu.VMEM)
    return pl.pallas_call(
        functools.partial(frame_kernel, pair),
        out_shape=jax.ShapeDtypeStruct((8, block * (2 if pair else 1), c), BF),
        in_specs=[pl.BlockSpec(memory_space=pltpu.SMEM)]
        + [vmem] * 9
        + [vmem if pair else pl.BlockSpec(memory_space=pl.ANY)],
        out_specs=vmem,
        scratch_shapes=[pltpu.VMEM((tokens, c), BF)] * 3,
        compiler_params=pltpu.CompilerParams(vmem_limit_bytes=VMEM_LIMIT),
        cost_estimate=pl.CostEstimate(
            flops=8 * tokens * c * c + 4 * tokens * tokens * c,
            bytes_accessed=4 * 2**20,
            transcendentals=tokens * tokens,
        ),
        name="frame_attention",
    )(place, *xs, weights, other)


def by_cell(o):
    return (o & 7) * 32 + ((o >> 3) & 3) * 8 + (o >> 5)


def by_frame(o):
    return (o & 7) * 32 + (o >> 3)


def project_time(x, w_ref):
    values = x.astype(F32)
    average = jnp.mean(values, axis=-1, keepdims=True)
    centered = values - average
    spread = jnp.mean(centered * centered, axis=-1, keepdims=True)
    normed = (centered * lax.rsqrt(spread + EPS)).astype(BF)
    return [mm(normed, w_ref[i]).astype(BF) for i in range(3)]


def time_kernel(x_ref, bias_ref, w_ref, out_ref, x_s, q_s, k_s, v_s):
    c = x_ref.shape[-1]
    order = one_hot_rows(256, by_cell)
    for u in range(8):
        span = slice(32 * u, 32 * u + 32)
        x = mm(order, x_ref[:, span, :].reshape(256, c)).astype(BF)
        for ref, value in zip((x_s, q_s, k_s, v_s), [x, *project_time(x, w_ref)]):
            ref[:, span, :] = value.reshape(8, 32, c)
    for cell in range(8):
        scores = mm_nt(q_s[cell], k_s[cell]) * (c ** (-0.5) * LOG2E) + bias_ref[...]
        q_s[cell] = mm(softmax_rows(scores, 1.0), v_s[cell]).astype(BF)
    back = one_hot_rows(256, by_frame)
    for u in range(8):
        span = slice(32 * u, 32 * u + 32)
        y = mm(q_s[:, span, :].reshape(256, c), w_ref[3])
        y = (y + x_s[:, span, :].reshape(256, c).astype(F32)).astype(BF)
        out_ref[span] = mm(back, y).astype(BF).reshape(32, 4, 2, c)


def time_attention(x, bias, weights):
    r, tc, c = x.shape
    vmem = pl.BlockSpec(memory_space=pltpu.VMEM)
    return pl.pallas_call(
        time_kernel,
        out_shape=jax.ShapeDtypeStruct((256, 4, 2, c), BF),
        in_specs=[vmem] * 3,
        out_specs=vmem,
        scratch_shapes=[pltpu.VMEM((8, 256, c), BF)] * 4,
        compiler_params=pltpu.CompilerParams(vmem_limit_bytes=24 * 2**20),
        cost_estimate=pl.CostEstimate(
            flops=8 * r * tc * c * c + 8 * 4 * 256 * 256 * c,
            bytes_accessed=6 * 2**20,
            transcendentals=8 * 256 * 256,
        ),
        name="time_attention",
    )(x, bias, weights)


def shards(video, video_ids, w_space, w_time, spatial_attn, time_attn):
    frames, rows, cols, c = video.shape
    tm_count, rows_count = lax.axis_size("tm"), lax.axis_size("rows")
    half = frames // 2
    tokens = rows * cols
    me = lax.axis_index("rows")
    around = lambda a, by: lax.ppermute(
        a, "rows", [(i, (i + by) % rows_count) for i in range(rows_count)]
    )

    up = lax.ppermute(video[:, rows - 1], "rows", [(i, i + 1) for i in range(rows_count - 1)])
    dn = lax.ppermute(video[:, 0], "rows", [(i + 1, i) for i in range(rows_count - 1)])
    x = video.reshape(frames, tokens, c)
    inner = conv_inner(x, w_space)

    ids = jnp.concatenate([jnp.full((2,), -1, jnp.int32), video_ids])
    ids = lax.dynamic_slice_in_dim(ids, lax.axis_index("tm") * frames, frames + 2)
    place = jnp.arange(frames, dtype=jnp.int32) % half
    one = jnp.where(ids[1:-1] == ids[2:], place + 1, place + 2)
    two = jnp.where(ids[:-2] == ids[2:], place, one)

    def slots(late):
        own = slice(half, frames) if late else slice(0, half)
        first = half if late else 0
        table = jnp.stack([place[own] + 2, one[own], two[own], place[own] + first])
        return lax.dynamic_slice_in_dim(jnp.concatenate([table, table], axis=1), me, half, axis=1)

    *late, lead, tail = conv_outer(True, slots(True), x, up, dn, inner, [], w_space, w_time)
    tail = lax.ppermute(tail, "tm", [(t, t + 1) for t in range(tm_count - 1)])
    early = conv_outer(False, slots(False), x, up, dn, inner, [lead, tail], w_space, w_time)

    sources = lax.rem(me - jnp.arange(rows_count, dtype=jnp.int32) + rows_count, rows_count)
    def exchanged(conv):
        return [conv[0]] + [around(conv[s], s) for s in range(1, rows_count)]

    done = frame_attention(False, sources, exchanged(late), spatial_attn, early[0])
    done = frame_attention(True, sources, exchanged(early), spatial_attn, done)
    arrived = lax.all_to_all(
        done.reshape(rows_count * tm_count, -1, c), ("rows", "tm"), 0, 0, tiled=True
    ).reshape(rows_count, -1, c)

    number = jnp.arange(frames * tm_count, dtype=jnp.int32)
    allowed = (number[None, :] <= number[:, None]) & (video_ids[None, :] == video_ids[:, None])
    return time_attention(arrived, jnp.where(allowed, 0.0, MASKED).astype(F32), time_attn)


def solution(mesh):
    in_specs = (P("tm", "rows", None, None), P(), P(), P(), P(), P())
    out_specs = P(None, "rows", "tm", None)
    return jax.shard_map(shards, mesh=mesh, in_specs=in_specs, out_specs=out_specs, check_vma=False)
```

```python
import functools

import jax
import jax.numpy as jnp
from jax import lax
from jax.experimental import pallas as pl
from jax.experimental.pallas import tpu as pltpu
from jax.sharding import Mesh, PartitionSpec as P

GROUPS = 32
EPS = 1e-06
MASKED = -1e30
LOG2E = 1.4426950408889634
BF = jnp.bfloat16
F32 = jnp.float32
VMEM_LIMIT = 16 * 1024 * 1024


def mm(a, b):
    return jnp.dot(a, b, preferred_element_type=F32)


def mm_nt(a, b):
    return lax.dot_general(a, b, (((1,), (1,)), ((), ())), preferred_element_type=F32)


def one_hot_rows(n, source_of):
    out_row = lax.broadcasted_iota(jnp.int32, (n, n), 0)
    in_row = lax.broadcasted_iota(jnp.int32, (n, n), 1)
    return jnp.where(in_row == source_of(out_row), 1.0, 0.0).astype(BF)


def space_taps(blocks, rows, lhs_of, w_ref, acc, store):
    c = acc.shape[-1]
    row = lax.broadcasted_iota(jnp.int32, (rows, c), 0) & 31

    def product(block, col):
        weights = jnp.concatenate([w_ref[3 * a + col] for a in range(3)], axis=0)
        return mm(lhs_of(block), weights)

    def span(block):
        return slice(block * rows, (block + 1) * rows)

    for block in range(blocks):
        acc[span(block)] = jnp.where(row == 0, 0.0, pltpu.roll(product(block, 0), 1, 0))
    for block in range(blocks):
        acc[span(block)] += product(block, 1)
    for block in range(blocks):
        v = acc[span(block)] + jnp.where(row == 31, 0.0, pltpu.roll(product(block, 2), rows - 1, 0))
        half = 0.5 * v
        store(block, (half + half * jnp.tanh(half)).astype(BF))


def inner_kernel(x_ref, w_ref, out_ref, acc):
    frames, tokens, c = out_ref.shape
    per = 8

    def lhs_of(block):
        f = slice(block * per, (block + 1) * per)
        return jnp.concatenate(
            [x_ref[f, 32 * a : 32 * a + tokens, :].reshape(per * tokens, c) for a in range(3)], axis=1
        )

    def store(block, hidden):
        out_ref[block * per : (block + 1) * per] = hidden.reshape(per, tokens, c)

    space_taps(frames // per, per * tokens, lhs_of, w_ref, acc, store)


def conv_inner(x, w_space):
    frames, tokens, c = x.shape
    rows = frames * (tokens - 64)
    vmem = pl.BlockSpec(memory_space=pltpu.VMEM)
    return pl.pallas_call(
        inner_kernel,
        out_shape=jax.ShapeDtypeStruct((frames, tokens - 64, c), BF),
        in_specs=[vmem] * 2,
        out_specs=vmem,
        scratch_shapes=[pltpu.VMEM((rows, c), F32)],
        compiler_params=pltpu.CompilerParams(vmem_limit_bytes=VMEM_LIMIT),
        cost_estimate=pl.CostEstimate(flops=18 * rows * c * c, bytes_accessed=8 * 2**20, transcendentals=0),
        name="conv_inner",
    )(x, w_space)


def outer_kernel(late, idx_ref, x_ref, up_ref, dn_ref, inner_ref, *refs):
    tokens, c = x_ref.shape[1:]
    count = 10 if late else 6
    frames = slice(6, 16) if late else slice(0, 6)
    if late:
        (w_ref, wt_ref, *outs, lead_ref, tail_ref, acc, hs) = refs
        here = slice(0, 10)
    else:
        (lead_ref, tail_ref, w_ref, wt_ref, *outs, acc, hs) = refs
        here = slice(2, 8)
    rows = count * 64

    hs[here, 32:96, :] = inner_ref[frames]
    if not late:
        hs[0:2] = tail_ref[...]
        hs[8:10] = lead_ref[...]

    def lhs_of(block):
        first = [up_ref[frames], x_ref[frames, 0:32, :], x_ref[frames, 32:64, :]]
        last = [x_ref[frames, 64:96, :], x_ref[frames, 96:128, :], dn_ref[frames]]
        return jnp.concatenate(
            [jnp.concatenate([f, l], axis=0).reshape(rows, c) for f, l in zip(first, last)], axis=1
        )

    def store(block, hidden):
        hidden = hidden.reshape(2, count, 32, c)
        hs[here, 0:32, :] = hidden[0]
        hs[here, 96:128, :] = hidden[1]

    space_taps(1, rows, lhs_of, w_ref, acc, store)

    order = one_hot_rows(128, lambda o: ((o >> 1) & 3) * 32 + (o >> 3) * 2 + (o & 1))
    weights = wt_ref[...].reshape(3 * c, c)
    per = 4
    for s0 in range(0, 8, per):
        taps = [jnp.concatenate([hs[idx_ref[k, s0 + s]] for s in range(per)], axis=0) for k in range(3)]
        y = mm(jnp.concatenate(taps, axis=1), weights)
        for s in range(per):
            own = y[s * tokens : (s + 1) * tokens] + x_ref[idx_ref[3, s0 + s]].astype(F32)
            k = s0 + s
            outs[k // 2][(k % 2) * tokens : (k % 2 + 1) * tokens] = mm(order, own.astype(BF)).astype(BF)
    if late:
        lead_ref[...] = hs[0:2]
        tail_ref[...] = hs[8:10]


def conv_outer(late, idx, x, up, dn, inner, given, w_space, w_time):
    tokens, c = x.shape[1:]
    count = 10 if late else 6
    ins = [x, up, dn, inner, *given, w_space, w_time]
    vmem = pl.BlockSpec(memory_space=pltpu.VMEM)
    out_shape = [jax.ShapeDtypeStruct((2 * tokens, c), BF)] * 4
    if late:
        out_shape = out_shape + [jax.ShapeDtypeStruct((2, tokens, c), BF)] * 2
    rows = count * 64
    return pl.pallas_call(
        functools.partial(outer_kernel, late),
        out_shape=out_shape,
        in_specs=[pl.BlockSpec(memory_space=pltpu.SMEM)] + [vmem] * len(ins),
        out_specs=[vmem] * len(out_shape),
        scratch_shapes=[pltpu.VMEM((rows, c), F32), pltpu.VMEM((10, tokens, c), BF)],
        compiler_params=pltpu.CompilerParams(vmem_limit_bytes=VMEM_LIMIT),
        cost_estimate=pl.CostEstimate(
            flops=18 * rows * c * c + 48 * tokens * c * c, bytes_accessed=9 * 2**20, transcendentals=0
        ),
        name="conv_outer",
    )(idx, *ins)


def softmax_rows(scores, scale):
    top = jnp.max(scores, axis=-1, keepdims=True)
    raised = jnp.exp2((scores - top) * scale)
    return (raised * (1.0 / jnp.sum(raised, axis=-1, keepdims=True))).astype(BF)


def group_sum(v, per_group):
    lane = lax.broadcasted_iota(jnp.int32, v.shape, 1)
    n = v.shape[1]
    d = 1
    while d < per_group:
        v = v + jnp.where((lane & d) == 0, pltpu.roll(v, n - d, 1), pltpu.roll(v, d, 1))
        d *= 2
    return v


def frame_kernel(pair, place_ref, *refs):
    owns, (twins_ref, w_ref, other_ref, out_ref, x_s, q_s, k_s, v_s) = refs[:4], refs[4:]
    block, c = twins_ref.shape[1:]
    rows = 2 * block
    tokens = 4 * rows
    per_group = c // GROUPS
    entries = tokens * per_group

    sums, squares = 0.0, 0.0
    for s in range(4):
        x = jnp.concatenate([owns[s][0:block], twins_ref[s]], axis=0)
        x_s[s * rows : (s + 1) * rows] = x
        values = x.astype(F32)
        sums = sums + jnp.sum(values, axis=0, keepdims=True)
        squares = squares + jnp.sum(values * values, axis=0, keepdims=True)
    both = group_sum(jnp.concatenate([sums, squares] * 4, axis=0), per_group) / entries
    average, square = both[0:1], both[1:2]
    inverse = lax.rsqrt(square - average * average + EPS)
    for s in range(4):
        span = slice(s * rows, (s + 1) * rows)
        normed = ((x_s[span].astype(F32) - average) * inverse).astype(BF)
        for i, ref in enumerate((q_s, k_s, v_s)):
            ref[span] = mm(normed, w_ref[i]).astype(BF)
    spans = [slice(s * rows, (s + 1) * rows) for s in range(4)]
    scores = [mm_nt(q_s[span], k_s[...]) for span in spans]
    probs = [softmax_rows(s, c ** (-0.5) * LOG2E) for s in scores]
    mixes = [mm(p, v_s[...]).astype(BF) for p in probs]
    for s in range(4):
        y = mm(mixes[s], w_ref[3]) + x_s[spans[s]].astype(F32)
        for core in range(2):
            part = y[core * block : (core + 1) * block]
            place = place_ref[core, s]
            if pair:
                other = other_ref[place].astype(F32).reshape(block // 8, 8, c)
                part = jnp.concatenate([part.reshape(block // 8, 8, c), other], axis=1)
            out_ref[place] = part.reshape(-1, c).astype(BF)


def frame_attention(pair, place, owns, twins, weights, other):
    block, c = twins.shape[1:]
    tokens = 8 * block
    vmem = pl.BlockSpec(memory_space=pltpu.VMEM)
    return pl.pallas_call(
        functools.partial(frame_kernel, pair),
        out_shape=jax.ShapeDtypeStruct((8, block * (2 if pair else 1), c), BF),
        in_specs=[pl.BlockSpec(memory_space=pltpu.SMEM)]
        + [vmem] * 6
        + [vmem if pair else pl.BlockSpec(memory_space=pl.ANY)],
        out_specs=vmem,
        scratch_shapes=[pltpu.VMEM((tokens, c), BF)] * 4,
        compiler_params=pltpu.CompilerParams(vmem_limit_bytes=VMEM_LIMIT),
        cost_estimate=pl.CostEstimate(
            flops=8 * tokens * c * c + 4 * tokens * tokens * c,
            bytes_accessed=4 * 2**20,
            transcendentals=tokens * tokens,
        ),
        name="frame_attention",
    )(place, *owns, twins, weights, other)


def by_cell(o):
    return (o & 7) * 32 + ((o >> 3) & 3) * 8 + (o >> 5)


def by_frame(o):
    return (o & 7) * 32 + (o >> 3)


def project_time(x, w_ref):
    values = x.astype(F32)
    average = jnp.mean(values, axis=-1, keepdims=True)
    centered = values - average
    spread = jnp.mean(centered * centered, axis=-1, keepdims=True)
    normed = (centered * lax.rsqrt(spread + EPS)).astype(BF)
    return [mm(normed, w_ref[i]).astype(BF) for i in range(3)]


def time_kernel(x_ref, bias_ref, w_ref, out_ref, x_s, q_s, k_s, v_s):
    c = x_ref.shape[-1]
    spans = [slice(32 * u, 32 * u + 32) for u in range(8)]
    order, back = one_hot_rows(256, by_cell), one_hot_rows(256, by_frame)
    for span in spans:
        x_s[:, span, :] = mm(order, x_ref[:, span, :].reshape(256, c)).astype(BF).reshape(8, 32, c)
    for span in spans:
        parts = project_time(x_s[:, span, :].reshape(256, c), w_ref)
        for ref, value in zip((q_s, k_s, v_s), parts):
            ref[:, span, :] = value.reshape(8, 32, c)
    scores = [mm_nt(q_s[i], k_s[i]) * (c ** (-0.5) * LOG2E) + bias_ref[...] for i in range(8)]
    probs = [softmax_rows(s, 1.0) for s in scores]
    for i in range(8):
        q_s[i] = mm(probs[i], v_s[i]).astype(BF)
    for span in spans:
        y = mm(q_s[:, span, :].reshape(256, c), w_ref[3])
        y = (y + x_s[:, span, :].reshape(256, c).astype(F32)).astype(BF)
        k_s[:, span, :] = y.reshape(8, 32, c)
    for span in spans:
        out_ref[span] = mm(back, k_s[:, span, :].reshape(256, c)).astype(BF).reshape(32, 4, 2, c)


def time_attention(x, bias, weights):
    r, tc, c = x.shape
    vmem = pl.BlockSpec(memory_space=pltpu.VMEM)
    return pl.pallas_call(
        time_kernel,
        out_shape=jax.ShapeDtypeStruct((256, 4, 2, c), BF),
        in_specs=[vmem] * 3,
        out_specs=vmem,
        scratch_shapes=[pltpu.VMEM((8, 256, c), BF)] * 4,
        compiler_params=pltpu.CompilerParams(vmem_limit_bytes=24 * 2**20),
        cost_estimate=pl.CostEstimate(
            flops=8 * r * tc * c * c + 8 * 4 * 256 * 256 * c,
            bytes_accessed=6 * 2**20,
            transcendentals=8 * 256 * 256,
        ),
        name="time_attention",
    )(x, bias, weights)


def shards(video, video_ids, w_space, w_time, spatial_attn, time_attn):
    frames, rows, cols, c = video.shape
    tm_count, y_count = lax.axis_size("tm"), lax.axis_size("y")
    half = frames // 2
    tokens = rows * cols
    y, core = lax.axis_index("y"), lax.axis_index("core")
    row_axes = ("y", "core")
    row_count = 2 * y_count
    swapped = lambda a: lax.ppermute(a, "core", [(0, 1), (1, 0)])

    up = lax.ppermute(video[:, rows - 1], row_axes, [(i, i + 1) for i in range(row_count - 1)])
    dn = lax.ppermute(video[:, 0], row_axes, [(i + 1, i) for i in range(row_count - 1)])
    x = video.reshape(frames, tokens, c)
    inner = conv_inner(x, w_space)

    ids = jnp.concatenate([jnp.full((2,), -1, jnp.int32), video_ids])
    ids = lax.dynamic_slice_in_dim(ids, lax.axis_index("tm") * frames, frames + 2)
    place = jnp.arange(frames, dtype=jnp.int32) % half
    one = jnp.where(ids[1:-1] == ids[2:], place + 1, place + 2)
    two = jnp.where(ids[:-2] == ids[2:], place, one)
    steps = jnp.arange(y_count, dtype=jnp.int32)
    ahead = 2 * lax.rem(y + steps, y_count)
    goes = jnp.stack([ahead + core, ahead + 1 - core], axis=1).reshape(-1)
    behind = 2 * lax.rem(y - steps + y_count, y_count)
    place_of = jnp.stack([behind + core, behind + 1 - core])

    def slots(late):
        own = slice(half, frames) if late else slice(0, half)
        first = half if late else 0
        table = jnp.stack([place[own] + 2, one[own], two[own], place[own] + first])
        chosen = goes[:, None] == jnp.arange(half, dtype=jnp.int32)[None, :]
        return jnp.sum(jnp.where(chosen[None], table[:, None, :], 0), axis=2)

    def exchanged(blocks):
        turn = lambda s: [(i, (i + s) % y_count) for i in range(y_count)]
        owns = [blocks[0]] + [lax.ppermute(blocks[s], "y", turn(s)) for s in range(1, y_count)]
        return owns, swapped(jnp.stack([a[tokens:] for a in owns]))

    *late, lead, tail = conv_outer(True, slots(True), x, up, dn, inner, [], w_space, w_time)
    tail = lax.ppermute(tail, "tm", [(t, t + 1) for t in range(tm_count - 1)])
    early = conv_outer(False, slots(False), x, up, dn, inner, [lead, tail], w_space, w_time)

    done = frame_attention(False, place_of, *exchanged(late), spatial_attn, early[0])
    done = frame_attention(True, place_of, *exchanged(early), spatial_attn, done)
    arrived = lax.all_to_all(
        done.reshape(row_count * tm_count, -1, c), ("y", "core", "tm"), 0, 0, tiled=True
    ).reshape(row_count, -1, c)

    number = jnp.arange(frames * tm_count, dtype=jnp.int32)
    allowed = (number[None, :] <= number[:, None]) & (video_ids[None, :] == video_ids[:, None])
    return time_attention(arrived, jnp.where(allowed, 0.0, MASKED).astype(F32), time_attn)


def solution(mesh):
    mesh = Mesh(mesh.devices.reshape(mesh.devices.shape[0], -1, 2), ("tm", "y", "core"))
    rows = ("y", "core")
    in_specs = (P("tm", rows, None, None), P(), P(), P(), P(), P())
    out_specs = P(None, rows, "tm", None)
    return jax.shard_map(shards, mesh=mesh, in_specs=in_specs, out_specs=out_specs, check_vma=False)
```

```python
import functools

import jax
import jax.numpy as jnp
from jax import lax
from jax.experimental import pallas as pl
from jax.experimental.pallas import tpu as pltpu
from jax.sharding import Mesh, PartitionSpec as P

GROUPS = 32
EPS = 1e-06
MASKED = -1e30
LOG2E = 1.4426950408889634
BF = jnp.bfloat16
F32 = jnp.float32
VMEM_LIMIT = 16 * 1024 * 1024


def mm(a, b):
    return jnp.dot(a, b, preferred_element_type=F32)


def mm_nt(a, b):
    return lax.dot_general(a, b, (((1,), (1,)), ((), ())), preferred_element_type=F32)


def one_hot_rows(n, source_of):
    out_row = lax.broadcasted_iota(jnp.int32, (n, n), 0)
    in_row = lax.broadcasted_iota(jnp.int32, (n, n), 1)
    return jnp.where(in_row == source_of(out_row), 1.0, 0.0).astype(BF)


def space_taps(blocks, rows, lhs_of, w_of, acc, store):
    c = acc.shape[-1]
    row = lax.broadcasted_iota(jnp.int32, (rows, c), 0) & 31

    def product(block, weights):
        return mm(lhs_of(block), weights)

    def span(block):
        return slice(block * rows, (block + 1) * rows)

    weights = w_of(0)
    for block in range(blocks):
        acc[span(block)] = jnp.where(row == 0, 0.0, pltpu.roll(product(block, weights), 1, 0))
    weights = w_of(1)
    for block in range(blocks):
        acc[span(block)] += product(block, weights)
    weights = w_of(2)
    for block in range(blocks):
        v = acc[span(block)] + jnp.where(row == 31, 0.0, pltpu.roll(product(block, weights), rows - 1, 0))
        half = 0.5 * v
        store(block, (half + half * jnp.tanh(half)).astype(BF))


def inner_kernel(x_ref, w_ref, out_ref, acc, w_s, sems):
    frames, tokens, c = out_ref.shape
    per = 8
    copies = [pltpu.make_async_copy(w_ref.at[:, col], w_s.at[col], sems.at[col]) for col in range(3)]
    for copy in copies:
        copy.start()

    def w_of(col):
        copies[col].wait()
        return w_s[col].reshape(3 * c, c)

    def lhs_of(block):
        f = slice(block * per, (block + 1) * per)
        return jnp.concatenate(
            [x_ref[f, 32 * a : 32 * a + tokens, :].reshape(per * tokens, c) for a in range(3)], axis=1
        )

    def store(block, hidden):
        out_ref[block * per : (block + 1) * per] = hidden.reshape(per, tokens, c)

    space_taps(frames // per, per * tokens, lhs_of, w_of, acc, store)


def conv_inner(x, w_space):
    frames, tokens, c = x.shape
    rows = frames * (tokens - 64)
    vmem = pl.BlockSpec(memory_space=pltpu.VMEM)
    return pl.pallas_call(
        inner_kernel,
        out_shape=jax.ShapeDtypeStruct((frames, tokens - 64, c), BF),
        in_specs=[vmem, pl.BlockSpec(memory_space=pltpu.HBM)],
        out_specs=vmem,
        scratch_shapes=[
            pltpu.VMEM((rows, c), F32),
            pltpu.VMEM((3, 3, c, c), BF),
            pltpu.SemaphoreType.DMA((3,)),
        ],
        compiler_params=pltpu.CompilerParams(vmem_limit_bytes=VMEM_LIMIT),
        cost_estimate=pl.CostEstimate(flops=18 * rows * c * c, bytes_accessed=8 * 2**20, transcendentals=0),
        name="conv_inner",
    )(x, pltpu.with_memory_space_constraint(w_space.reshape(3, 3, c, c), pltpu.HBM))


def outer_kernel(late, idx_ref, x_ref, up_ref, dn_ref, inner_ref, *refs):
    tokens, c = x_ref.shape[1:]
    count = 10 if late else 6
    frames = slice(6, 16) if late else slice(0, 6)
    if late:
        (w_ref, wt_ref, *outs, lead_ref, tail_ref, acc, hs) = refs
        here = slice(0, 10)
    else:
        (lead_ref, tail_ref, w_ref, wt_ref, *outs, acc, hs) = refs
        here = slice(2, 8)
    rows = count * 64

    hs[here, 32:96, :] = inner_ref[frames]
    if not late:
        hs[0:2] = tail_ref[...]
        hs[8:10] = lead_ref[...]

    def lhs_of(block):
        first = [up_ref[frames], x_ref[frames, 0:32, :], x_ref[frames, 32:64, :]]
        last = [x_ref[frames, 64:96, :], x_ref[frames, 96:128, :], dn_ref[frames]]
        return jnp.concatenate(
            [jnp.concatenate([f, l], axis=0).reshape(rows, c) for f, l in zip(first, last)], axis=1
        )

    def store(block, hidden):
        hidden = hidden.reshape(2, count, 32, c)
        hs[here, 0:32, :] = hidden[0]
        hs[here, 96:128, :] = hidden[1]

    def w_of(col):
        return jnp.concatenate([w_ref[3 * a + col] for a in range(3)], axis=0)

    space_taps(1, rows, lhs_of, w_of, acc, store)

    order = one_hot_rows(128, lambda o: ((o >> 1) & 3) * 32 + (o >> 3) * 2 + (o & 1))
    weights = wt_ref[...].reshape(3 * c, c)
    per = 4
    for s0 in range(0, 8, per):
        taps = [jnp.concatenate([hs[idx_ref[k, s0 + s]] for s in range(per)], axis=0) for k in range(3)]
        y = mm(jnp.concatenate(taps, axis=1), weights)
        for s in range(per):
            own = y[s * tokens : (s + 1) * tokens] + x_ref[idx_ref[3, s0 + s]].astype(F32)
            k = s0 + s
            outs[k // 2][(k % 2) * tokens : (k % 2 + 1) * tokens] = mm(order, own.astype(BF)).astype(BF)
    if late:
        lead_ref[...] = hs[0:2]
        tail_ref[...] = hs[8:10]


def conv_outer(late, idx, x, up, dn, inner, given, w_space, w_time):
    tokens, c = x.shape[1:]
    count = 10 if late else 6
    ins = [x, up, dn, inner, *given, w_space, w_time]
    vmem = pl.BlockSpec(memory_space=pltpu.VMEM)
    out_shape = [jax.ShapeDtypeStruct((2 * tokens, c), BF)] * 4
    if late:
        out_shape = out_shape + [jax.ShapeDtypeStruct((2, tokens, c), BF)] * 2
    rows = count * 64
    return pl.pallas_call(
        functools.partial(outer_kernel, late),
        out_shape=out_shape,
        in_specs=[pl.BlockSpec(memory_space=pltpu.SMEM)] + [vmem] * len(ins),
        out_specs=[vmem] * len(out_shape),
        scratch_shapes=[pltpu.VMEM((rows, c), F32), pltpu.VMEM((10, tokens, c), BF)],
        compiler_params=pltpu.CompilerParams(vmem_limit_bytes=VMEM_LIMIT),
        cost_estimate=pl.CostEstimate(
            flops=18 * rows * c * c + 48 * tokens * c * c, bytes_accessed=9 * 2**20, transcendentals=0
        ),
        name="conv_outer",
    )(idx, *ins)


def softmax_rows(scores, scale):
    top = jnp.max(scores, axis=-1, keepdims=True)
    raised = jnp.exp2((scores - top) * scale)
    return (raised * (1.0 / jnp.sum(raised, axis=-1, keepdims=True))).astype(BF)


def group_sum(v, per_group):
    lane = lax.broadcasted_iota(jnp.int32, v.shape, 1)
    n = v.shape[1]
    d = 1
    while d < per_group:
        v = v + jnp.where((lane & d) == 0, pltpu.roll(v, n - d, 1), pltpu.roll(v, d, 1))
        d *= 2
    return v


def frame_kernel(pair, place_ref, *refs):
    owns, (twins_ref, w_ref, other_ref, out_ref, x_s, q_s, k_s, v_s) = refs[:4], refs[4:]
    block, c = twins_ref.shape[1:]
    rows = 2 * block
    tokens = 4 * rows
    per_group = c // GROUPS
    entries = tokens * per_group

    sums, squares = 0.0, 0.0
    for s in range(4):
        x = jnp.concatenate([owns[s][0:block], twins_ref[s]], axis=0)
        x_s[s * rows : (s + 1) * rows] = x
        values = x.astype(F32)
        sums = sums + jnp.sum(values, axis=0, keepdims=True)
        squares = squares + jnp.sum(values * values, axis=0, keepdims=True)
    both = group_sum(jnp.concatenate([sums, squares] * 4, axis=0), per_group) / entries
    average, square = both[0:1], both[1:2]
    inverse = lax.rsqrt(square - average * average + EPS)
    for s in range(4):
        span = slice(s * rows, (s + 1) * rows)
        normed = ((x_s[span].astype(F32) - average) * inverse).astype(BF)
        for i, ref in enumerate((q_s, k_s, v_s)):
            ref[span] = mm(normed, w_ref[i]).astype(BF)
    spans = [slice(s * rows, (s + 1) * rows) for s in range(4)]
    scores = [mm_nt(q_s[span], k_s[...]) for span in spans]
    probs = [softmax_rows(s, c ** (-0.5) * LOG2E) for s in scores]
    mixes = [mm(p, v_s[...]).astype(BF) for p in probs]
    for s in range(4):
        y = mm(mixes[s], w_ref[3]) + x_s[spans[s]].astype(F32)
        for core in range(2):
            part = y[core * block : (core + 1) * block]
            place = place_ref[core, s]
            if pair:
                other = other_ref[place].astype(F32).reshape(block // 8, 8, c)
                part = jnp.concatenate([part.reshape(block // 8, 8, c), other], axis=1)
            out_ref[place] = part.reshape(-1, c).astype(BF)


def frame_attention(pair, place, owns, twins, weights, other):
    block, c = twins.shape[1:]
    tokens = 8 * block
    vmem = pl.BlockSpec(memory_space=pltpu.VMEM)
    return pl.pallas_call(
        functools.partial(frame_kernel, pair),
        out_shape=jax.ShapeDtypeStruct((8, block * (2 if pair else 1), c), BF),
        in_specs=[pl.BlockSpec(memory_space=pltpu.SMEM)]
        + [vmem] * 6
        + [vmem if pair else pl.BlockSpec(memory_space=pl.ANY)],
        out_specs=vmem,
        scratch_shapes=[pltpu.VMEM((tokens, c), BF)] * 4,
        compiler_params=pltpu.CompilerParams(vmem_limit_bytes=VMEM_LIMIT),
        cost_estimate=pl.CostEstimate(
            flops=8 * tokens * c * c + 4 * tokens * tokens * c,
            bytes_accessed=4 * 2**20,
            transcendentals=tokens * tokens,
        ),
        name="frame_attention",
    )(place, *owns, twins, weights, other)


def by_cell(o):
    return (o & 7) * 32 + ((o >> 3) & 3) * 8 + (o >> 5)


def by_frame(o):
    return (o & 7) * 32 + (o >> 3)


def project_time(x, w_ref):
    values = x.astype(F32)
    average = jnp.mean(values, axis=-1, keepdims=True)
    centered = values - average
    spread = jnp.mean(centered * centered, axis=-1, keepdims=True)
    normed = (centered * lax.rsqrt(spread + EPS)).astype(BF)
    return [mm(normed, w_ref[i]).astype(BF) for i in range(3)]


def time_kernel(x_ref, bias_ref, w_ref, out_ref, x_s, q_s, k_s, v_s):
    c = x_ref.shape[-1]
    spans = [slice(32 * u, 32 * u + 32) for u in range(8)]
    order, back = one_hot_rows(256, by_cell), one_hot_rows(256, by_frame)
    for span in spans:
        x_s[:, span, :] = mm(order, x_ref[:, span, :].reshape(256, c)).astype(BF).reshape(8, 32, c)
    for span in spans:
        parts = project_time(x_s[:, span, :].reshape(256, c), w_ref)
        for ref, value in zip((q_s, k_s, v_s), parts):
            ref[:, span, :] = value.reshape(8, 32, c)
    scores = [mm_nt(q_s[i], k_s[i]) * (c ** (-0.5) * LOG2E) + bias_ref[...] for i in range(8)]
    probs = [softmax_rows(s, 1.0) for s in scores]
    for i in range(8):
        q_s[i] = mm(probs[i], v_s[i]).astype(BF)
    for span in spans:
        y = mm(q_s[:, span, :].reshape(256, c), w_ref[3])
        y = (y + x_s[:, span, :].reshape(256, c).astype(F32)).astype(BF)
        k_s[:, span, :] = y.reshape(8, 32, c)
    for span in spans:
        out_ref[span] = mm(back, k_s[:, span, :].reshape(256, c)).astype(BF).reshape(32, 4, 2, c)


def time_attention(x, bias, weights):
    r, tc, c = x.shape
    vmem = pl.BlockSpec(memory_space=pltpu.VMEM)
    return pl.pallas_call(
        time_kernel,
        out_shape=jax.ShapeDtypeStruct((256, 4, 2, c), BF),
        in_specs=[vmem] * 3,
        out_specs=vmem,
        scratch_shapes=[pltpu.VMEM((8, 256, c), BF)] * 4,
        compiler_params=pltpu.CompilerParams(vmem_limit_bytes=24 * 2**20),
        cost_estimate=pl.CostEstimate(
            flops=8 * r * tc * c * c + 8 * 4 * 256 * 256 * c,
            bytes_accessed=6 * 2**20,
            transcendentals=8 * 256 * 256,
        ),
        name="time_attention",
    )(x, bias, weights)


def shards(video, video_ids, w_space, w_time, spatial_attn, time_attn):
    frames, rows, cols, c = video.shape
    tm_count, y_count = lax.axis_size("tm"), lax.axis_size("y")
    half = frames // 2
    tokens = rows * cols
    y, core = lax.axis_index("y"), lax.axis_index("core")
    row_axes = ("y", "core")
    row_count = 2 * y_count
    swapped = lambda a: lax.ppermute(a, "core", [(0, 1), (1, 0)])

    up = lax.ppermute(video[:, rows - 1], row_axes, [(i, i + 1) for i in range(row_count - 1)])
    dn = lax.ppermute(video[:, 0], row_axes, [(i + 1, i) for i in range(row_count - 1)])
    x = video.reshape(frames, tokens, c)
    inner = conv_inner(x, w_space)

    ids = jnp.concatenate([jnp.full((2,), -1, jnp.int32), video_ids])
    ids = lax.dynamic_slice_in_dim(ids, lax.axis_index("tm") * frames, frames + 2)
    place = jnp.arange(frames, dtype=jnp.int32) % half
    one = jnp.where(ids[1:-1] == ids[2:], place + 1, place + 2)
    two = jnp.where(ids[:-2] == ids[2:], place, one)
    steps = jnp.arange(y_count, dtype=jnp.int32)
    ahead = 2 * lax.rem(y + steps, y_count)
    goes = jnp.stack([ahead + core, ahead + 1 - core], axis=1).reshape(-1)
    behind = 2 * lax.rem(y - steps + y_count, y_count)
    place_of = jnp.stack([behind + core, behind + 1 - core])

    def slots(late):
        own = slice(half, frames) if late else slice(0, half)
        first = half if late else 0
        table = jnp.stack([place[own] + 2, one[own], two[own], place[own] + first])
        chosen = goes[:, None] == jnp.arange(half, dtype=jnp.int32)[None, :]
        return jnp.sum(jnp.where(chosen[None], table[:, None, :], 0), axis=2)

    def exchanged(blocks):
        turn = lambda s: [(i, (i + s) % y_count) for i in range(y_count)]
        owns = [blocks[0]] + [lax.ppermute(blocks[s], "y", turn(s)) for s in range(1, y_count)]
        return owns, swapped(jnp.stack([a[tokens:] for a in owns]))

    *late, lead, tail = conv_outer(True, slots(True), x, up, dn, inner, [], w_space, w_time)
    tail = lax.ppermute(tail, "tm", [(t, t + 1) for t in range(tm_count - 1)])
    early = conv_outer(False, slots(False), x, up, dn, inner, [lead, tail], w_space, w_time)

    done = frame_attention(False, place_of, *exchanged(late), spatial_attn, early[0])
    done = frame_attention(True, place_of, *exchanged(early), spatial_attn, done)
    arrived = lax.all_to_all(
        done.reshape(row_count * tm_count, -1, c), ("y", "core", "tm"), 0, 0, tiled=True
    ).reshape(row_count, -1, c)

    number = jnp.arange(frames * tm_count, dtype=jnp.int32)
    allowed = (number[None, :] <= number[:, None]) & (video_ids[None, :] == video_ids[:, None])
    return time_attention(arrived, jnp.where(allowed, 0.0, MASKED).astype(F32), time_attn)


def solution(mesh):
    mesh = Mesh(mesh.devices.reshape(mesh.devices.shape[0], -1, 2), ("tm", "y", "core"))
    rows = ("y", "core")
    in_specs = (P("tm", rows, None, None), P(), P(), P(), P(), P())
    out_specs = P(None, rows, "tm", None)
    return jax.shard_map(shards, mesh=mesh, in_specs=in_specs, out_specs=out_specs, check_vma=False)
```
